32 devices in a mesh: outer: 2 (over y), rep: 4 (over x, core), tp: 4 (over z).
Axes of the slice: x: 2, y: 2, z: 4, core: 2. Of those that a mesh axis runs over, the one named last changes fastest.
Arguments:
- hidden: bfloat16 [16384, 8192], P(('outer', 'rep'), 'tp'), parts along dimension 0, may hold values from -2000 to 2000, as said below
- lengths: int32 [8], P('outer'), parts along dimension 0, may hold values from 1 to 16, 32 in all
- adapter_index: int32 [8], P('outer'), parts along dimension 0, may hold values from 0 to 3, as said below
- gain: float32 [8192], P('tp'), may hold values from 0.1 to 1.9
- wkv: bfloat16 [8192, 2048], P('tp'), may hold values from -0.09375 to 0.09375
- down_weights: bfloat16 [8192, 128], P('tp'), may hold values from -0.0625 to 0.0625
- key_up_weights: bfloat16 [64, 1024], replicated, may hold values from -1.5 to 1.5
- value_up_weights: bfloat16 [64, 1024], replicated, may hold values from -1.5 to 1.5
Outputs:
- kv_cache: bfloat16 [16384, 2048], P(('outer', 'rep'), 'tp'), parts along dimension 0
The draws below stay inside these ranges and needn't reach their ends.
There are 2 independent parts, one for each index of `outer`. The reference program is written for one: setup_inputs(seed, part) draws one part's arguments, and reference() takes and returns one part's arrays. A program takes and returns all parts, laid end to end along the dimension named above; an argument that names none is the same for every part. Nothing has to cross between parts.
Inputs may be any that keep to these rules, and one draw needn't show every extreme that they name: `hidden`: the layer's input activations. The lengths sum to exactly 32, and some owner fills all 16 slots. `adapter_index`: every adapter is named by some owner.
All inputs are finite; a program needn't handle non-finite values.
Results may differ from the reference program's by a relative error of at most 0.012.
Values may be sent and summed in bfloat16 or wider, within the bound.
A program may use at most 128 MiB of HBM per device.

```python
import math
import jax
import jax.numpy as jnp
import numpy as np
from jax import lax

MODEL_WIDTH = 8192
KEY_VALUE_HEADS = 8
HEAD_WIDTH = 128
SPAN = 128
ADAPTER_RANK = 16
ADAPTER_TOTAL = 4
SPAN_MEAN = 8
SLOTS = 16
OWNERS = 4
TOTAL_SPANS = 32
KVC = 2048
N_REP = 4
N_TP = 4


def draw_hidden(key, part):
    key = jax.random.fold_in(key, 11)
    first, second, third = jax.random.split(key, 3)
    row_count = OWNERS * SLOTS * SPAN
    base_projection = jnp.clip(jax.random.normal(first, (row_count, MODEL_WIDTH), jnp.float32), -4.0, 4.0)
    row_scale = jnp.exp(jax.random.uniform(second, (row_count, 1), jnp.float32) * jnp.log(10.0))
    ramp = jnp.sqrt(1.0 + 2.0 * jnp.arange(MODEL_WIDTH, dtype=jnp.float32) / (MODEL_WIDTH - 1))
    column_scale = jnp.exp(jax.random.uniform(third, (1, MODEL_WIDTH), jnp.float32) * jnp.log(10.0)) * ramp[None, :]
    return (base_projection * row_scale * column_scale).astype(jnp.bfloat16)


def draw_adapter_index(key, part):
    key = jax.random.fold_in(key, 23)
    owner_ids = jnp.arange(OWNERS, dtype=jnp.int32)
    drawn = jax.random.randint(key, (OWNERS,), 0, ADAPTER_TOTAL, dtype=jnp.int32)
    part_number = jnp.asarray(part, dtype=jnp.int32)
    rotated = jnp.mod(owner_ids + part_number, ADAPTER_TOTAL).astype(jnp.int32)
    return jnp.where(owner_ids < ADAPTER_TOTAL, rotated, drawn).astype(jnp.int32)


def strengthened(values, stream_key, source, target, parts, factor):
    def block_of(position):
        return (jnp.arange(values.shape[position]) // (values.shape[position] // parts)).reshape((-1,) + (1,) * (values.ndim - 1 - position))

    one_side = jax.random.permutation(stream_key, parts)[block_of(target)]
    far = (block_of(target) + parts // 2) % parts
    return jnp.where((block_of(source) == one_side) | (block_of(source) == far), factor * values, values)


def block_scale(stream_key, dims, pieces, least, high):
    level = 1.0
    for dim, blocks in pieces:
        draws = jax.random.uniform(jax.random.fold_in(jax.random.fold_in(stream_key, 6), dim), (blocks,), jnp.float32, least / len(pieces), high / len(pieces))
        level = level * jnp.repeat(jnp.exp(draws), dims[dim] // blocks).reshape((-1,) + (1,) * (len(dims) - 1 - dim))
    return level


def length_profile(number_of, total, bound, slope):
    portions = [(1 << 20) // math.isqrt(standing ** slope) + 1 for standing in range(2, number_of + 1)]
    rest, given = total - bound - (number_of - 1), [1] * (number_of - 1)
    while rest > 0:
        candidates = [i for i in range(number_of - 1) if given[i] < bound]
        pool, budget = sum([portions[i] for i in candidates]), rest
        for i in candidates:
            more = min(bound - given[i], max(1, budget * portions[i] // pool), rest)
            given[i] = given[i] + more
            rest = rest - more
    return np.array([bound] + given)


def ragged_sizes(stream_key, number_of, total, bound, skew):
    if number_of == 2:
        one = jax.random.randint(stream_key, (), max(1, total - bound), min(bound, total - 1) + 1)
        return jnp.stack([one, total - one])
    tallies = jnp.asarray(length_profile(number_of, total, bound, skew), jnp.int32)
    couples = (number_of - 1) // 2
    donor, taker = tallies[1:1 + 2 * couples:2], tallies[2:2 + 2 * couples:2]
    room = jnp.minimum(donor - 1, bound - taker)
    shifted = jax.random.randint(jax.random.fold_in(stream_key, 1), (couples,), 0, 1 << 20) % (room + 1)
    tallies = tallies.at[1:1 + 2 * couples:2].set(donor - shifted).at[2:2 + 2 * couples:2].set(taker + shifted)
    return tallies[jax.random.permutation(jax.random.fold_in(stream_key, 2), number_of)]


def gaussian(own_key, shape, spread, limit, cuts=(), held_as=jnp.bfloat16):
    factor_of = block_scale(own_key, shape, cuts, -0.22, 0.18) if cuts else 1.0
    entries = jax.random.normal(own_key, shape, jnp.float32) * spread * factor_of
    return jnp.minimum(jnp.maximum(entries, -limit), limit).astype(held_as)


def heavy_noise(rng, dims, width, bound, shards, heavy, kind=jnp.bfloat16):
    array = width * jax.random.normal(rng, dims, jnp.float32)
    if shards:
        array = array * block_scale(rng, dims, shards, -0.22, 0.18)
    return jnp.clip(strengthened(array, jax.random.fold_in(rng, 3), *heavy), -bound, bound).astype(kind)


def setup_inputs(seed: int = 0, part: int = 0) -> dict:
    key_of = jax.random.split(jax.random.key(seed), 9)
    part_splits = jax.random.split(jax.random.fold_in(key_of[8], part), 9)
    hidden = draw_hidden(jax.random.fold_in(jax.random.fold_in(key_of[8], part), 71), part)
    lengths = ragged_sizes(part_splits[1], OWNERS, TOTAL_SPANS, SLOTS, 2).astype(jnp.int32)
    adapter_index = draw_adapter_index(jax.random.fold_in(jax.random.fold_in(key_of[8], part), 71), part)
    gain = jnp.clip(1.0 + 0.18 * jax.random.normal(key_of[3], (MODEL_WIDTH,), jnp.float32), 0.1, 1.9)
    wkv = heavy_noise(key_of[4], (MODEL_WIDTH, KVC), MODEL_WIDTH ** -0.5, 0.09375, ((0, 4),), (0, 1, 4, 2.0))
    down_weights = gaussian(key_of[5], (MODEL_WIDTH, ADAPTER_TOTAL * 2 * ADAPTER_RANK), MODEL_WIDTH ** -0.5, 0.0625, ((0, 4),))
    key_up_weights = gaussian(key_of[6], (ADAPTER_TOTAL * ADAPTER_RANK, KEY_VALUE_HEADS * HEAD_WIDTH), ADAPTER_RANK ** -0.5, 1.5)
    value_up_weights = gaussian(key_of[7], (ADAPTER_TOTAL * ADAPTER_RANK, KEY_VALUE_HEADS * HEAD_WIDTH), ADAPTER_RANK ** -0.5, 1.5)
    return {"hidden": hidden, "lengths": lengths, "adapter_index": adapter_index, "gain": gain, "wkv": wkv, "down_weights": down_weights, "key_up_weights": key_up_weights, "value_up_weights": value_up_weights}


EPSILON = 1e-05
THETA = 500000.0
ADAPTER_SCALE = 0.5

def rotate_keys(keys, positions):
    head_size = keys.shape[-1]
    half = head_size // 2
    index = jnp.arange(half, dtype=jnp.float32)
    inverse = jnp.power(jnp.float32(THETA), -2.0 * index / head_size)
    angles = positions.astype(jnp.float32)[:, None] * inverse[None, :]
    cosine = jnp.concatenate([jnp.cos(angles), jnp.cos(angles)], axis=1)
    sine = jnp.concatenate([jnp.sin(angles), jnp.sin(angles)], axis=1)
    turned = jnp.concatenate([-keys[..., half:], keys[..., :half]], axis=-1)
    return keys * cosine[:, None, :] + turned * sine[:, None, :]

def local_partial_sum(scaled_part, adapter_rows_used, weight_part, down_part, key_up_matrix, value_up_matrix):
    row_count = scaled_part.shape[0]
    key_column_count = key_up_matrix.shape[1]
    base_projection = jnp.dot(scaled_part, weight_part, preferred_element_type=jnp.float32)
    low_rank = jnp.dot(scaled_part, down_part, preferred_element_type=jnp.float32)
    adapter_count = key_up_matrix.shape[0] // ADAPTER_RANK
    selector = (adapter_rows_used[:, None] == jnp.arange(adapter_count, dtype=jnp.int32)[None, :]).astype(jnp.float32)
    low_rank = low_rank.reshape(row_count, adapter_count, 2, ADAPTER_RANK) * selector[:, :, None, None]
    reduced_key_rank = low_rank[:, :, 0, :].reshape(row_count, adapter_count * ADAPTER_RANK).astype(jnp.bfloat16)
    reduced_value_rank = low_rank[:, :, 1, :].reshape(row_count, adapter_count * ADAPTER_RANK).astype(jnp.bfloat16)
    adapter_key_delta = jnp.dot(reduced_key_rank, key_up_matrix, preferred_element_type=jnp.float32)
    adapter_value_delta = jnp.dot(reduced_value_rank, value_up_matrix, preferred_element_type=jnp.float32)
    return jnp.concatenate([base_projection[:, :key_column_count] + ADAPTER_SCALE * adapter_key_delta, base_projection[:, key_column_count:] + ADAPTER_SCALE * adapter_value_delta], axis=1)

def reference(hidden, lengths, adapter_index, gain, wkv, down_weights, key_up_weights, value_up_weights):
    span_ends = jnp.cumsum(lengths).astype(jnp.int32)
    starts = (span_ends - lengths).astype(jnp.int32)
    total_count = SPAN_MEAN * N_REP
    global_index = jnp.arange(total_count, dtype=jnp.int32)
    owners = lax.optimization_barrier(jnp.sum((global_index[:, None] >= span_ends[None, :]).astype(jnp.int32), axis=1)).astype(jnp.int32)
    slots = (global_index - starts[owners]).astype(jnp.int32)
    flat_index = (owners * SLOTS + slots).astype(jnp.int32)
    span_rows = hidden.reshape(N_REP * SLOTS, SPAN, MODEL_WIDTH)
    span_portion = MODEL_WIDTH // N_TP

    def recompute(item):
        index_block, slot_block, owner_block = item
        rows_here = jnp.take(span_rows, index_block, axis=0).reshape(SPAN_MEAN * SPAN, MODEL_WIDTH)
        positions = (slot_block[:, None] * SPAN + jnp.arange(SPAN, dtype=jnp.int32)[None, :]).reshape(-1)
        adapter_rows_used = jnp.repeat(adapter_index[owner_block], SPAN)
        values = rows_here.astype(jnp.float32)
        inverse_rms = lax.rsqrt(lax.optimization_barrier(jnp.mean(values * values, axis=1)) + EPSILON)
        scaled_delta = (values * gain).astype(jnp.bfloat16)
        summed = jnp.zeros((SPAN_MEAN * SPAN, KVC), jnp.float32)
        for shard_number in range(N_TP):
            down_projected = shard_number * span_portion
            part = local_partial_sum(scaled_delta[:, down_projected:down_projected + span_portion], adapter_rows_used, wkv[down_projected:down_projected + span_portion], down_weights[down_projected:down_projected + span_portion], key_up_weights, value_up_weights)
            rounded = lax.optimization_barrier(part.astype(jnp.bfloat16))
            summed = summed + rounded.astype(jnp.float32)
        normed = summed * inverse_rms[:, None]
        keys = rotate_keys(normed[:, :KEY_VALUE_HEADS * HEAD_WIDTH].reshape(-1, KEY_VALUE_HEADS, HEAD_WIDTH), positions).reshape(-1, KEY_VALUE_HEADS * HEAD_WIDTH)
        result = jnp.concatenate([keys, normed[:, KEY_VALUE_HEADS * HEAD_WIDTH:]], axis=1).astype(jnp.bfloat16)
        return result.reshape(SPAN_MEAN, SPAN, KVC)
    results = lax.map(recompute, (flat_index.reshape(N_REP, SPAN_MEAN), slots.reshape(N_REP, SPAN_MEAN), owners.reshape(N_REP, SPAN_MEAN)))
    output = jnp.zeros((N_REP * SLOTS, SPAN, KVC), jnp.bfloat16).at[flat_index].set(results.reshape(total_count, SPAN, KVC))
    return output.reshape(N_REP * SLOTS * SPAN, KVC)
```

```python
import jax
import jax.numpy as jnp
from jax import lax
from jax.sharding import PartitionSpec as P

MODEL_WIDTH = 8192
KEY_VALUE_HEADS = 8
HEAD_WIDTH = 128
SPAN = 128
ADAPTER_RANK = 16
SLOTS = 16

EPSILON = 1e-05
THETA = 500000.0
ADAPTER_SCALE = 0.5


def rotate_keys(keys, positions):
    head_size = keys.shape[-1]
    half = head_size // 2
    index = jnp.arange(half, dtype=jnp.float32)
    inverse = jnp.power(jnp.float32(THETA), -2.0 * index / head_size)
    angles = positions.astype(jnp.float32)[:, None] * inverse[None, :]
    cosine = jnp.concatenate([jnp.cos(angles), jnp.cos(angles)], axis=1)
    sine = jnp.concatenate([jnp.sin(angles), jnp.sin(angles)], axis=1)
    turned = jnp.concatenate([-keys[..., half:], keys[..., :half]], axis=-1)
    return keys * cosine[:, None, :] + turned * sine[:, None, :]


def body(hidden, lengths, adapter_index, gain, wkv, down_weights, key_up_weights, value_up_weights):
    my_replica = lax.axis_index("rep")
    my_shard = lax.axis_index("tp")
    shards = lax.axis_size("tp")
    own_length = lengths[my_replica]
    adapter = adapter_index[my_replica]
    key_columns = key_up_weights.shape[1]
    column_width = wkv.shape[1] // shards
    rank = ADAPTER_RANK
    down_own = lax.dynamic_slice_in_dim(down_weights, adapter * 2 * rank, 2 * rank, 1)
    key_up = lax.dynamic_slice_in_dim(key_up_weights, adapter * rank, rank, 0)
    value_up = lax.dynamic_slice_in_dim(value_up_weights, adapter * rank, rank, 0)
    up = jnp.concatenate(
        [
            jnp.concatenate([key_up, jnp.zeros_like(key_up)], axis=1),
            jnp.concatenate([jnp.zeros_like(value_up), value_up], axis=1),
        ],
        axis=0,
    )
    chunks = 4
    rows = SLOTS * SPAN // chunks
    outputs = []
    for c in range(chunks):
        part = lax.slice_in_dim(hidden, c * rows, (c + 1) * rows, axis=0)
        values = part.astype(jnp.float32)
        squares = lax.psum(jnp.sum(values * values, axis=1), "tp")
        scaled = (values * gain).astype(jnp.bfloat16)
        low = jnp.dot(scaled, down_own, preferred_element_type=jnp.float32).astype(jnp.bfloat16)
        partial = jnp.dot(scaled, wkv, preferred_element_type=jnp.float32)
        partial = partial + ADAPTER_SCALE * jnp.dot(low, up, preferred_element_type=jnp.float32)
        summed = lax.psum_scatter(
            partial.astype(jnp.bfloat16), "tp", scatter_dimension=1, tiled=True
        ).astype(jnp.float32)
        normed = summed * lax.rsqrt(squares / MODEL_WIDTH + EPSILON)[:, None]
        positions = c * rows + jnp.arange(rows, dtype=jnp.int32)
        turned = rotate_keys(
            normed.reshape(rows, column_width // HEAD_WIDTH, HEAD_WIDTH), positions
        ).reshape(rows, column_width)
        is_key = my_shard * column_width < key_columns
        result = jnp.where(is_key, turned, normed)
        live = positions < own_length * SPAN
        outputs.append(jnp.where(live[:, None], result, 0.0).astype(jnp.bfloat16))
    return jnp.concatenate(outputs, axis=0)


def solution(mesh):
    return jax.shard_map(
        body,
        mesh=mesh,
        in_specs=(
            P(("outer", "rep"), "tp"),
            P("outer"),
            P("outer"),
            P("tp"),
            P("tp", None),
            P("tp", None),
            P(),
            P(),
        ),
        out_specs=P(("outer", "rep"), "tp"),
        check_vma=False,
    )
```

```python
import functools

import jax
import jax.numpy as jnp
from jax import lax
from jax.experimental import pallas as pl
from jax.experimental.pallas import tpu as pltpu
from jax.sharding import PartitionSpec as P

MODEL_WIDTH = 8192
KEY_VALUE_HEADS = 8
HEAD_WIDTH = 128
SPAN = 128
ADAPTER_RANK = 16
SLOTS = 16

EPSILON = 1e-05
THETA = 500000.0
ADAPTER_SCALE = 0.5


def rotate_keys(keys, positions):
    head_size = keys.shape[-1]
    half = head_size // 2
    index = jnp.arange(half, dtype=jnp.float32)
    inverse = jnp.power(jnp.float32(THETA), -2.0 * index / head_size)
    angles = positions.astype(jnp.float32)[:, None] * inverse[None, :]
    cosine = jnp.concatenate([jnp.cos(angles), jnp.cos(angles)], axis=1)
    sine = jnp.concatenate([jnp.sin(angles), jnp.sin(angles)], axis=1)
    turned = jnp.concatenate([-keys[..., half:], keys[..., :half]], axis=-1)
    return keys * cosine[:, None, :] + turned * sine[:, None, :]


def kernel(
    n, blocks, rows, columns,
    hidden, gain, wkv, down, up, summed, square_sums,
    scaled, partial, from_left, from_right, squares,
    right_send, right_recv, left_send, left_recv, square_send, square_recv,
):
    me = lax.axis_index("tp")
    right, left = lax.rem(me + 1, n), lax.rem(me + n - 1, n)
    mesh_id = pl.DeviceIdType.MESH

    barrier = pltpu.get_barrier_semaphore()

    @pl.loop(0, n)
    def _(peer):
        @pl.when(peer != me)
        def _():
            pl.semaphore_signal(barrier, inc=1, device_id={"tp": peer}, device_id_type=mesh_id)

    pl.semaphore_wait(barrier, n - 1)

    def rightward(b, j):
        return pltpu.make_async_remote_copy(
            src_ref=partial.at[b, j], dst_ref=from_left.at[b, j],
            send_sem=right_send.at[b, j], recv_sem=right_recv.at[b, j],
            device_id={"tp": right}, device_id_type=mesh_id,
        )

    def leftward(b, j):
        return pltpu.make_async_remote_copy(
            src_ref=partial.at[b, j], dst_ref=from_right.at[b, j],
            send_sem=left_send.at[b, j], recv_sem=left_recv.at[b, j],
            device_id={"tp": left}, device_id_type=mesh_id,
        )

    def square_copy(source, peer):
        return pltpu.make_async_remote_copy(
            src_ref=squares.at[source], dst_ref=squares.at[source],
            send_sem=square_send.at[peer], recv_sem=square_recv.at[source],
            device_id={"tp": peer}, device_id_type=mesh_id,
        )

    def add_arrived(b, j, arrived):
        partial[b, j] = (
            partial[b, j].astype(jnp.float32) + arrived[b, j].astype(jnp.float32)
        ).astype(jnp.bfloat16)

    ones = jnp.ones((8, hidden.shape[1]), jnp.bfloat16)
    over_width = (((1,), (1,)), ((), ()))

    @pl.loop(0, blocks)
    def _(b):
        values = hidden[pl.ds(b * rows, rows), :].astype(jnp.float32)
        scaled[...] = (values * gain[...]).astype(jnp.bfloat16)
        square = values * values
        high = square.astype(jnp.bfloat16)
        low = (square - high.astype(jnp.float32)).astype(jnp.bfloat16)
        squares[me, :, pl.ds(b * rows, rows)] = lax.dot_general(
            ones, high, over_width, preferred_element_type=jnp.float32
        ) + lax.dot_general(ones, low, over_width, preferred_element_type=jnp.float32)
        low_rank = jnp.dot(
            scaled[...], down[...], preferred_element_type=jnp.float32
        ).astype(jnp.bfloat16)

        @pl.loop(0, n)
        def _(j):
            here = pl.ds(pl.multiple_of(j * columns, columns), columns)
            base = jnp.dot(scaled[...], wkv[:, here], preferred_element_type=jnp.float32)
            delta = jnp.dot(low_rank, up[:, here], preferred_element_type=jnp.float32)
            partial[b, j] = (base + ADAPTER_SCALE * delta).astype(jnp.bfloat16)

        @pl.when(me == 0)
        def _():
            @pl.loop(1, n)
            def _(j):
                rightward(b, n - j).start()

        @pl.when(me == n - 1)
        def _():
            @pl.loop(0, n - 1)
            def _(j):
                leftward(b, j).start()

    @pl.loop(0, n)
    def _(peer):
        @pl.when(peer != me)
        def _():
            square_copy(me, peer).start()

    @pl.loop(0, blocks + 1)
    def _(step):
        @pl.when(step < blocks)
        def _():
            b = step

            @pl.when((me > 0) & (me < n - 1))
            def _():
                @pl.loop(0, n)
                def _(i):
                    j = n - 1 - i

                    @pl.when(j > me)
                    def _():
                        rightward(b, j).wait_recv()
                        add_arrived(b, j, from_left)
                        rightward(b, j).start()

                    @pl.when(i < me)
                    def _():
                        leftward(b, i).wait_recv()
                        add_arrived(b, i, from_right)
                        leftward(b, i).start()

        @pl.when(step > 0)
        def _():
            b = step - 1

            @pl.when(me > 0)
            def _():
                rightward(b, me).wait_recv()
                add_arrived(b, me, from_left)

            @pl.when(me < n - 1)
            def _():
                leftward(b, me).wait_recv()
                add_arrived(b, me, from_right)

            summed[pl.ds(b * rows, rows), :] = partial[b, me]

    @pl.loop(0, n)
    def _(peer):
        @pl.when(peer != me)
        def _():
            square_copy(peer, peer).wait_recv()
            square_copy(me, peer).wait_send()

    total = squares[0]
    for peer in range(1, n):
        total = total + squares[peer]
    square_sums[...] = total

    @pl.loop(0, blocks)
    def _(b):
        @pl.loop(0, n)
        def _(j):
            @pl.when(j > me)
            def _():
                rightward(b, j).wait_send()

            @pl.when(j < me)
            def _():
                leftward(b, j).wait_send()


def body(hidden, lengths, adapter_index, gain, wkv, down_weights, key_up_weights, value_up_weights):
    my_replica = lax.axis_index("rep")
    my_shard = lax.axis_index("tp")
    n = lax.axis_size("tp")
    own_length = lengths[my_replica]
    adapter = adapter_index[my_replica]
    key_columns = key_up_weights.shape[1]
    width = hidden.shape[1]
    row_count = hidden.shape[0]
    columns = wkv.shape[1] // n
    adapters = key_up_weights.shape[0] // ADAPTER_RANK
    mine = (jnp.arange(adapters) == adapter)[:, None, None]
    key_up = jnp.where(mine, key_up_weights.reshape(adapters, ADAPTER_RANK, -1), 0)
    value_up = jnp.where(mine, value_up_weights.reshape(adapters, ADAPTER_RANK, -1), 0)
    up = jnp.concatenate(
        [
            jnp.concatenate([key_up, jnp.zeros_like(value_up)], axis=2),
            jnp.concatenate([jnp.zeros_like(key_up), value_up], axis=2),
        ],
        axis=1,
    ).reshape(down_weights.shape[1], wkv.shape[1])
    rows = 2 * SPAN
    blocks = row_count // rows
    vmem = pl.BlockSpec(memory_space=pltpu.VMEM)
    chunk_buffer = pltpu.VMEM((blocks, n, rows, columns), jnp.bfloat16)
    chunk_semaphores = pltpu.SemaphoreType.DMA((blocks, n))
    summed, square_sums = pl.pallas_call(
        functools.partial(kernel, n, blocks, rows, columns),
        out_shape=(
            jax.ShapeDtypeStruct((row_count, columns), jnp.bfloat16),
            jax.ShapeDtypeStruct((8, row_count), jnp.float32),
        ),
        in_specs=[vmem] * 5,
        out_specs=(vmem, vmem),
        scratch_shapes=[
            pltpu.VMEM((rows, width), jnp.bfloat16),
            chunk_buffer,
            chunk_buffer,
            chunk_buffer,
            pltpu.VMEM((n, 8, row_count), jnp.float32),
            chunk_semaphores,
            chunk_semaphores,
            chunk_semaphores,
            chunk_semaphores,
            pltpu.SemaphoreType.DMA((n,)),
            pltpu.SemaphoreType.DMA((n,)),
        ],
        compiler_params=pltpu.CompilerParams(
            collective_id=0, has_side_effects=True, vmem_limit_bytes=60 * 1024 * 1024
        ),
    )(hidden, gain[None, :], wkv, down_weights, up)
    inverse_rms = lax.rsqrt(square_sums[0] / MODEL_WIDTH + EPSILON)
    normed = summed.astype(jnp.float32) * inverse_rms[:, None]
    positions = jnp.arange(row_count, dtype=jnp.int32)
    turned = rotate_keys(
        normed.reshape(row_count, columns // HEAD_WIDTH, HEAD_WIDTH), positions
    ).reshape(row_count, columns)
    is_key = my_shard * columns < key_columns
    live = positions < own_length * SPAN
    result = jnp.where(is_key, turned, normed)
    return jnp.where(live[:, None], result, 0.0).astype(jnp.bfloat16)


def solution(mesh):
    return jax.shard_map(
        body,
        mesh=mesh,
        in_specs=(
            P(("outer", "rep"), "tp"),
            P("outer"),
            P("outer"),
            P("tp"),
            P("tp", None),
            P("tp", None),
            P(),
            P(),
        ),
        out_specs=P(("outer", "rep"), "tp"),
        check_vma=False,
    )
```

```python
import functools

import jax
import jax.numpy as jnp
from jax import lax
from jax.experimental import pallas as pl
from jax.experimental.pallas import tpu as pltpu
from jax.sharding import PartitionSpec as P

MODEL_WIDTH = 8192
KEY_VALUE_HEADS = 8
HEAD_WIDTH = 128
SPAN = 128
ADAPTER_RANK = 16
SLOTS = 16

EPSILON = 1e-05
THETA = 500000.0
ADAPTER_SCALE = 0.5


def kernel(
    n, blocks, rows, columns, key_columns,
    hidden, gain, wkv, down, up, frequency, limit, result, scaled, cosine, sine, partial, from_left, from_right, squares,
    right_send, right_recv, left_send, left_recv, square_send, square_recv,
):
    me = lax.axis_index("tp")
    right, left = lax.rem(me + 1, n), lax.rem(me + n - 1, n)
    mesh_id = pl.DeviceIdType.MESH

    barrier = pltpu.get_barrier_semaphore()

    @pl.loop(0, n)
    def _(peer):
        @pl.when(peer != me)
        def _():
            pl.semaphore_signal(barrier, inc=1, device_id={"tp": peer}, device_id_type=mesh_id)

    pl.semaphore_wait(barrier, n - 1)

    def rightward(b, j):
        return pltpu.make_async_remote_copy(
            src_ref=partial.at[b, j], dst_ref=from_left.at[b, j],
            send_sem=right_send.at[b, j], recv_sem=right_recv.at[b, j],
            device_id={"tp": right}, device_id_type=mesh_id,
        )

    def leftward(b, j):
        return pltpu.make_async_remote_copy(
            src_ref=partial.at[b, j], dst_ref=from_right.at[b, j],
            send_sem=left_send.at[b, j], recv_sem=left_recv.at[b, j],
            device_id={"tp": left}, device_id_type=mesh_id,
        )

    def square_copy(source, peer):
        return pltpu.make_async_remote_copy(
            src_ref=squares.at[source], dst_ref=squares.at[source],
            send_sem=square_send.at[peer], recv_sem=square_recv.at[source],
            device_id={"tp": peer}, device_id_type=mesh_id,
        )

    def add_arrived(b, j, arrived):
        partial[b, j] = (
            partial[b, j].astype(jnp.float32) + arrived[b, j].astype(jnp.float32)
        ).astype(jnp.bfloat16)

    ones = jnp.ones((8, hidden.shape[1]), jnp.bfloat16)
    over_width = (((1,), (1,)), ((), ()))

    @pl.loop(0, blocks)
    def _(b):
        values = hidden[pl.ds(b * rows, rows), :].astype(jnp.float32)
        scaled[...] = (values * gain[...]).astype(jnp.bfloat16)
        square = values * values
        high = square.astype(jnp.bfloat16)
        low = (square - high.astype(jnp.float32)).astype(jnp.bfloat16)
        squares[me, :, pl.ds(b * rows, rows)] = lax.dot_general(
            ones, high, over_width, preferred_element_type=jnp.float32
        ) + lax.dot_general(ones, low, over_width, preferred_element_type=jnp.float32)
        low_rank = jnp.dot(
            scaled[...], down[...], preferred_element_type=jnp.float32
        ).astype(jnp.bfloat16)

        @pl.loop(0, n)
        def _(j):
            here = pl.ds(pl.multiple_of(j * columns, columns), columns)
            base = jnp.dot(scaled[...], wkv[:, here], preferred_element_type=jnp.float32)
            delta = jnp.dot(low_rank, up[:, here], preferred_element_type=jnp.float32)
            partial[b, j] = (base + ADAPTER_SCALE * delta).astype(jnp.bfloat16)

        @pl.when(me == 0)
        def _():
            @pl.loop(1, n)
            def _(j):
                rightward(b, n - j).start()

        @pl.when(me == n - 1)
        def _():
            @pl.loop(0, n - 1)
            def _(j):
                leftward(b, j).start()

    @pl.loop(0, n)
    def _(peer):
        @pl.when(peer != me)
        def _():
            square_copy(me, peer).start()

    @pl.loop(0, blocks + 1)
    def _(step):
        @pl.when(step < blocks)
        def _():
            b = step
            here = pl.ds(b * rows, rows)
            place = lax.broadcasted_iota(jnp.int32, (rows, HEAD_WIDTH), 0) + b * rows
            lane = lax.broadcasted_iota(jnp.int32, (rows, HEAD_WIDTH), 1)
            angles = place.astype(jnp.float32) * frequency[...]
            is_key = me * columns < key_columns
            cosine[here, :] = jnp.where(is_key, jnp.cos(angles), 1.0)
            turn = jnp.sin(angles)
            turn = jnp.where(lane < HEAD_WIDTH // 2, -turn, turn)
            sine[here, :] = jnp.where(is_key, turn, 0.0)

            @pl.when((me > 0) & (me < n - 1))
            def _():
                @pl.loop(0, n)
                def _(i):
                    j = n - 1 - i

                    @pl.when(j > me)
                    def _():
                        rightward(b, j).wait_recv()
                        add_arrived(b, j, from_left)
                        rightward(b, j).start()

                    @pl.when(i < me)
                    def _():
                        leftward(b, i).wait_recv()
                        add_arrived(b, i, from_right)
                        leftward(b, i).start()

        @pl.when(step > 0)
        def _():
            b = step - 1

            @pl.when(me > 0)
            def _():
                rightward(b, me).wait_recv()
                add_arrived(b, me, from_left)

            @pl.when(me < n - 1)
            def _():
                leftward(b, me).wait_recv()
                add_arrived(b, me, from_right)

    @pl.loop(0, n)
    def _(peer):
        @pl.when(peer != me)
        def _():
            square_copy(peer, peer).wait_recv()
            square_copy(me, peer).wait_send()

    @pl.loop(0, blocks)
    def _(b):
        here = pl.ds(b * rows, rows)
        total = squares[0, :, here]
        for peer in range(1, n):
            total = total + squares[peer, :, here]
        inverse_rms = jnp.transpose(lax.rsqrt(total / MODEL_WIDTH + EPSILON))[:, 0:1]
        place = lax.broadcasted_iota(jnp.int32, (rows, HEAD_WIDTH), 0) + b * rows
        live = place < limit[...]
        for head in range(columns // HEAD_WIDTH):
            own = slice(head * HEAD_WIDTH, (head + 1) * HEAD_WIDTH)
            normed = partial[b, me, :, own].astype(jnp.float32) * inverse_rms
            turned = pltpu.roll(normed, HEAD_WIDTH // 2, 1)
            rotated = normed * cosine[here, :] + turned * sine[here, :]
            result[here, own] = jnp.where(live, rotated, 0.0).astype(jnp.bfloat16)

    @pl.loop(0, blocks)
    def _(b):
        @pl.loop(0, n)
        def _(j):
            @pl.when(j > me)
            def _():
                rightward(b, j).wait_send()

            @pl.when(j < me)
            def _():
                leftward(b, j).wait_send()


def body(hidden, lengths, adapter_index, gain, wkv, down_weights, key_up_weights, value_up_weights):
    my_replica = lax.axis_index("rep")
    n = lax.axis_size("tp")
    own_length = lengths[my_replica]
    adapter = adapter_index[my_replica]
    key_columns = key_up_weights.shape[1]
    width = hidden.shape[1]
    row_count = hidden.shape[0]
    columns = wkv.shape[1] // n
    adapters = key_up_weights.shape[0] // ADAPTER_RANK
    mine = (jnp.arange(adapters) == adapter)[:, None, None]
    key_up = jnp.where(mine, key_up_weights.reshape(adapters, ADAPTER_RANK, -1), 0)
    value_up = jnp.where(mine, value_up_weights.reshape(adapters, ADAPTER_RANK, -1), 0)
    up = jnp.concatenate(
        [
            jnp.concatenate([key_up, jnp.zeros_like(value_up)], axis=2),
            jnp.concatenate([jnp.zeros_like(key_up), value_up], axis=2),
        ],
        axis=1,
    ).reshape(down_weights.shape[1], wkv.shape[1])
    rows = 2 * SPAN
    blocks = row_count // rows
    vmem = pl.BlockSpec(memory_space=pltpu.VMEM)
    chunk_buffer = pltpu.VMEM((blocks, n, rows, columns), jnp.bfloat16)
    chunk_semaphores = pltpu.SemaphoreType.DMA((blocks, n))
    index = jnp.arange(HEAD_WIDTH // 2, dtype=jnp.float32)
    frequency = jnp.tile(jnp.power(jnp.float32(THETA), -2.0 * index / HEAD_WIDTH), 2)[None, :]
    limit = jnp.full((1, HEAD_WIDTH), own_length * SPAN, jnp.int32)
    return pl.pallas_call(
        functools.partial(kernel, n, blocks, rows, columns, key_columns),
        out_shape=jax.ShapeDtypeStruct((row_count, columns), jnp.bfloat16),
        in_specs=[vmem] * 7,
        out_specs=vmem,
        scratch_shapes=[
            pltpu.VMEM((rows, width), jnp.bfloat16),
            pltpu.VMEM((row_count, HEAD_WIDTH), jnp.float32),
            pltpu.VMEM((row_count, HEAD_WIDTH), jnp.float32),
            chunk_buffer,
            chunk_buffer,
            chunk_buffer,
            pltpu.VMEM((n, 8, row_count), jnp.float32),
            chunk_semaphores,
            chunk_semaphores,
            chunk_semaphores,
            chunk_semaphores,
            pltpu.SemaphoreType.DMA((n,)),
            pltpu.SemaphoreType.DMA((n,)),
        ],
        compiler_params=pltpu.CompilerParams(
            collective_id=0, has_side_effects=True, vmem_limit_bytes=60 * 1024 * 1024
        ),
    )(hidden, gain[None, :], wkv, down_weights, up, frequency, limit)


def solution(mesh):
    return jax.shard_map(
        body,
        mesh=mesh,
        in_specs=(
            P(("outer", "rep"), "tp"),
            P("outer"),
            P("outer"),
            P("tp"),
            P("tp", None),
            P("tp", None),
            P(),
            P(),
        ),
        out_specs=P(("outer", "rep"), "tp"),
        check_vma=False,
    )
```

```python
import functools

import jax
import jax.numpy as jnp
from jax import lax
from jax.experimental import pallas as pl
from jax.experimental.pallas import tpu as pltpu
from jax.sharding import PartitionSpec as P

MODEL_WIDTH = 8192
KEY_VALUE_HEADS = 8
HEAD_WIDTH = 128
SPAN = 128
ADAPTER_RANK = 16
SLOTS = 16

EPSILON = 1e-05
THETA = 500000.0
ADAPTER_SCALE = 0.5


def kernel(
    n, blocks, rows, columns, key_columns,
    hidden, gain, wkv, down, up, frequency, limit, result, scaled, cosine, sine, partial, from_left, from_right, squares,
    right_send, right_recv, left_send, left_recv, square_send, square_recv,
):
    me = lax.axis_index("tp")
    right, left = lax.rem(me + 1, n), lax.rem(me + n - 1, n)
    mesh_id = pl.DeviceIdType.MESH

    barrier = pltpu.get_barrier_semaphore()

    @pl.loop(0, n)
    def _(peer):
        @pl.when(peer != me)
        def _():
            pl.semaphore_signal(barrier, inc=1, device_id={"tp": peer}, device_id_type=mesh_id)

    pl.semaphore_wait(barrier, n - 1)

    def rightward(b, j):
        return pltpu.make_async_remote_copy(
            src_ref=partial.at[b, j], dst_ref=from_left.at[b, j],
            send_sem=right_send.at[b, j], recv_sem=right_recv.at[b, j],
            device_id={"tp": right}, device_id_type=mesh_id,
        )

    def leftward(b, j):
        return pltpu.make_async_remote_copy(
            src_ref=partial.at[b, j], dst_ref=from_right.at[b, j],
            send_sem=left_send.at[b, j], recv_sem=left_recv.at[b, j],
            device_id={"tp": left}, device_id_type=mesh_id,
        )

    def square_copy(source, peer):
        return pltpu.make_async_remote_copy(
            src_ref=squares.at[source], dst_ref=squares.at[source],
            send_sem=square_send.at[peer], recv_sem=square_recv.at[source],
            device_id={"tp": peer}, device_id_type=mesh_id,
        )

    def add_arrived(b, j, arrived):
        partial[b, j] = (
            partial[b, j].astype(jnp.float32) + arrived[b, j].astype(jnp.float32)
        ).astype(jnp.bfloat16)

    ones = jnp.ones((8, hidden.shape[1]), jnp.bfloat16)
    over_width = (((1,), (1,)), ((), ()))

    def compute(b):
        values = hidden[pl.ds(b * rows, rows), :].astype(jnp.float32)
        scaled[...] = (values * gain[...]).astype(jnp.bfloat16)
        square = values * values
        high = square.astype(jnp.bfloat16)
        low = (square - high.astype(jnp.float32)).astype(jnp.bfloat16)
        squares[me, :, pl.ds(b * rows, rows)] = lax.dot_general(
            ones, high, over_width, preferred_element_type=jnp.float32
        ) + lax.dot_general(ones, low, over_width, preferred_element_type=jnp.float32)
        low_rank = jnp.dot(
            scaled[...], down[...], preferred_element_type=jnp.float32
        ).astype(jnp.bfloat16)

        @pl.loop(0, n)
        def _(j):
            here = pl.ds(pl.multiple_of(j * columns, columns), columns)
            base = jnp.dot(scaled[...], wkv[:, here], preferred_element_type=jnp.float32)
            delta = jnp.dot(low_rank, up[:, here], preferred_element_type=jnp.float32)
            partial[b, j] = (base + ADAPTER_SCALE * delta).astype(jnp.bfloat16)

        @pl.when(me == 0)
        def _():
            @pl.loop(1, n)
            def _(j):
                rightward(b, n - j).start()

        @pl.when(me == n - 1)
        def _():
            @pl.loop(0, n - 1)
            def _(j):
                leftward(b, j).start()

    early = blocks // 2

    @pl.loop(0, blocks + early)
    def _(step):
        @pl.when(step < early)
        def _():
            @pl.loop(0, 2)
            def _(which):
                compute(2 * step + which)

        @pl.when(step == early - 1)
        def _():
            @pl.loop(0, n)
            def _(peer):
                @pl.when(peer != me)
                def _():
                    square_copy(me, peer).start()

        @pl.when(step < blocks)
        def _():
            b = step
            here = pl.ds(b * rows, rows)
            place = lax.broadcasted_iota(jnp.int32, (rows, HEAD_WIDTH), 0) + b * rows
            lane = lax.broadcasted_iota(jnp.int32, (rows, HEAD_WIDTH), 1)
            angles = place.astype(jnp.float32) * frequency[...]
            is_key = me * columns < key_columns
            cosine[here, :] = jnp.where(is_key, jnp.cos(angles), 1.0)
            turn = jnp.sin(angles)
            turn = jnp.where(lane < HEAD_WIDTH // 2, -turn, turn)
            sine[here, :] = jnp.where(is_key, turn, 0.0)

            @pl.when((me > 0) & (me < n - 1))
            def _():
                @pl.loop(0, n)
                def _(i):
                    j = n - 1 - i

                    @pl.when(j > me)
                    def _():
                        rightward(b, j).wait_recv()
                        add_arrived(b, j, from_left)
                        rightward(b, j).start()

                    @pl.when(i < me)
                    def _():
                        leftward(b, i).wait_recv()
                        add_arrived(b, i, from_right)
                        leftward(b, i).start()

        @pl.when(step >= early)
        def _():
            b = step - early

            @pl.when(me > 0)
            def _():
                rightward(b, me).wait_recv()
                add_arrived(b, me, from_left)

            @pl.when(me < n - 1)
            def _():
                leftward(b, me).wait_recv()
                add_arrived(b, me, from_right)

    @pl.loop(0, n)
    def _(peer):
        @pl.when(peer != me)
        def _():
            square_copy(peer, peer).wait_recv()
            square_copy(me, peer).wait_send()

    @pl.loop(0, blocks)
    def _(b):
        here = pl.ds(b * rows, rows)
        total = squares[0, :, here]
        for peer in range(1, n):
            total = total + squares[peer, :, here]
        inverse_rms = jnp.transpose(lax.rsqrt(total / MODEL_WIDTH + EPSILON))[:, 0:1]
        place = lax.broadcasted_iota(jnp.int32, (rows, HEAD_WIDTH), 0) + b * rows
        live = place < limit[...]
        for head in range(columns // HEAD_WIDTH):
            own = slice(head * HEAD_WIDTH, (head + 1) * HEAD_WIDTH)
            normed = partial[b, me, :, own].astype(jnp.float32) * inverse_rms
            turned = pltpu.roll(normed, HEAD_WIDTH // 2, 1)
            rotated = normed * cosine[here, :] + turned * sine[here, :]
            result[here, own] = jnp.where(live, rotated, 0.0).astype(jnp.bfloat16)

    @pl.loop(0, blocks)
    def _(b):
        @pl.loop(0, n)
        def _(j):
            @pl.when(j > me)
            def _():
                rightward(b, j).wait_send()

            @pl.when(j < me)
            def _():
                leftward(b, j).wait_send()


def body(hidden, lengths, adapter_index, gain, wkv, down_weights, key_up_weights, value_up_weights):
    my_replica = lax.axis_index("rep")
    n = lax.axis_size("tp")
    own_length = lengths[my_replica]
    adapter = adapter_index[my_replica]
    key_columns = key_up_weights.shape[1]
    width = hidden.shape[1]
    row_count = hidden.shape[0]
    columns = wkv.shape[1] // n
    adapters = key_up_weights.shape[0] // ADAPTER_RANK
    mine = (jnp.arange(adapters) == adapter)[:, None, None]
    key_up = jnp.where(mine, key_up_weights.reshape(adapters, ADAPTER_RANK, -1), 0)
    value_up = jnp.where(mine, value_up_weights.reshape(adapters, ADAPTER_RANK, -1), 0)
    up = jnp.concatenate(
        [
            jnp.concatenate([key_up, jnp.zeros_like(value_up)], axis=2),
            jnp.concatenate([jnp.zeros_like(key_up), value_up], axis=2),
        ],
        axis=1,
    ).reshape(down_weights.shape[1], wkv.shape[1])
    rows = 2 * SPAN
    blocks = row_count // rows
    vmem = pl.BlockSpec(memory_space=pltpu.VMEM)
    chunk_buffer = pltpu.VMEM((blocks, n, rows, columns), jnp.bfloat16)
    chunk_semaphores = pltpu.SemaphoreType.DMA((blocks, n))
    index = jnp.arange(HEAD_WIDTH // 2, dtype=jnp.float32)
    frequency = jnp.tile(jnp.power(jnp.float32(THETA), -2.0 * index / HEAD_WIDTH), 2)[None, :]
    limit = jnp.full((1, HEAD_WIDTH), own_length * SPAN, jnp.int32)
    return pl.pallas_call(
        functools.partial(kernel, n, blocks, rows, columns, key_columns),
        out_shape=jax.ShapeDtypeStruct((row_count, columns), jnp.bfloat16),
        in_specs=[vmem] * 7,
        out_specs=vmem,
        scratch_shapes=[
            pltpu.VMEM((rows, width), jnp.bfloat16),
            pltpu.VMEM((row_count, HEAD_WIDTH), jnp.float32),
            pltpu.VMEM((row_count, HEAD_WIDTH), jnp.float32),
            chunk_buffer,
            chunk_buffer,
            chunk_buffer,
            pltpu.VMEM((n, 8, row_count), jnp.float32),
            chunk_semaphores,
            chunk_semaphores,
            chunk_semaphores,
            chunk_semaphores,
            pltpu.SemaphoreType.DMA((n,)),
            pltpu.SemaphoreType.DMA((n,)),
        ],
        compiler_params=pltpu.CompilerParams(
            collective_id=0, has_side_effects=True, vmem_limit_bytes=60 * 1024 * 1024
        ),
    )(hidden, gain[None, :], wkv, down_weights, up, frequency, limit)


def solution(mesh):
    return jax.shard_map(
        body,
        mesh=mesh,
        in_specs=(
            P(("outer", "rep"), "tp"),
            P("outer"),
            P("outer"),
            P("tp"),
            P("tp", None),
            P("tp", None),
            P(),
            P(),
        ),
        out_specs=P(("outer", "rep"), "tp"),
        check_vma=False,
    )
```

```python
import functools

import jax
import jax.numpy as jnp
from jax import lax
from jax.experimental import pallas as pl
from jax.experimental.pallas import tpu as pltpu
from jax.sharding import PartitionSpec as P

MODEL_WIDTH = 8192
KEY_VALUE_HEADS = 8
HEAD_WIDTH = 128
SPAN = 128
ADAPTER_RANK = 16
SLOTS = 16

EPSILON = 1e-05
THETA = 500000.0
ADAPTER_SCALE = 0.5


def kernel(
    n, blocks, rows, columns, key_columns,
    hidden, gain, wkv, down, up, frequency, limit, result, scaled, cosine, sine, partial, from_left, from_right, squares,
    right_send, right_recv, left_send, left_recv, square_send, square_recv,
):
    me = lax.axis_index("tp")
    right, left = lax.rem(me + 1, n), lax.rem(me + n - 1, n)
    mesh_id = pl.DeviceIdType.MESH

    barrier = pltpu.get_barrier_semaphore()

    @pl.loop(0, n)
    def _(peer):
        @pl.when(peer != me)
        def _():
            pl.semaphore_signal(barrier, inc=1, device_id={"tp": peer}, device_id_type=mesh_id)

    pl.semaphore_wait(barrier, n - 1)

    def rightward(b, j):
        return pltpu.make_async_remote_copy(
            src_ref=partial.at[b, j], dst_ref=from_left.at[b, j],
            send_sem=right_send.at[b, j], recv_sem=right_recv.at[b, j],
            device_id={"tp": right}, device_id_type=mesh_id,
        )

    def leftward(b, j):
        return pltpu.make_async_remote_copy(
            src_ref=partial.at[b, j], dst_ref=from_right.at[b, j],
            send_sem=left_send.at[b, j], recv_sem=left_recv.at[b, j],
            device_id={"tp": left}, device_id_type=mesh_id,
        )

    def square_copy(source, peer):
        return pltpu.make_async_remote_copy(
            src_ref=squares.at[source], dst_ref=squares.at[source],
            send_sem=square_send.at[peer], recv_sem=square_recv.at[source],
            device_id={"tp": peer}, device_id_type=mesh_id,
        )

    def add_arrived(b, j, arrived):
        partial[b, j] = (
            partial[b, j].astype(jnp.float32) + arrived[b, j].astype(jnp.float32)
        ).astype(jnp.bfloat16)

    ones = jnp.ones((8, hidden.shape[1]), jnp.bfloat16)
    over_width = (((1,), (1,)), ((), ()))

    is_first = (n - 1 - me) // (n - 1)

    def compute(b):
        values = hidden[pl.ds(b * rows, rows), :].astype(jnp.float32)
        scaled[...] = (values * gain[...]).astype(jnp.bfloat16)
        low_rank = jnp.dot(
            scaled[...], down[...], preferred_element_type=jnp.float32
        ).astype(jnp.bfloat16)

        @pl.loop(0, n)
        def _(i):
            j = i + is_first * (n - 1 - 2 * i)
            here = pl.ds(pl.multiple_of(j * columns, columns), columns)
            base = jnp.dot(scaled[...], wkv[:, here], preferred_element_type=jnp.float32)
            delta = jnp.dot(low_rank, up[:, here], preferred_element_type=jnp.float32)
            partial[b, j] = (base + ADAPTER_SCALE * delta).astype(jnp.bfloat16)

            @pl.when((me == 0) & (j > 0))
            def _():
                rightward(b, j).start()

            @pl.when((me == n - 1) & (j < n - 1))
            def _():
                leftward(b, j).start()

        values = hidden[pl.ds(b * rows, rows), :].astype(jnp.float32)
        square = values * values
        high = square.astype(jnp.bfloat16)
        low = (square - high.astype(jnp.float32)).astype(jnp.bfloat16)
        squares[me, :, pl.ds(b * rows, rows)] = lax.dot_general(
            ones, high, over_width, preferred_element_type=jnp.float32
        ) + lax.dot_general(ones, low, over_width, preferred_element_type=jnp.float32)

    early = blocks // 2

    @pl.loop(0, blocks + early)
    def _(step):
        @pl.when(step < early)
        def _():
            @pl.loop(0, 2)
            def _(which):
                compute(2 * step + which)

        @pl.when(step == early - 1)
        def _():
            @pl.loop(0, n)
            def _(peer):
                @pl.when(peer != me)
                def _():
                    square_copy(me, peer).start()

        @pl.when(step < blocks)
        def _():
            b = step
            here = pl.ds(b * rows, rows)
            place = lax.broadcasted_iota(jnp.int32, (rows, HEAD_WIDTH), 0) + b * rows
            lane = lax.broadcasted_iota(jnp.int32, (rows, HEAD_WIDTH), 1)
            angles = place.astype(jnp.float32) * frequency[...]
            is_key = me * columns < key_columns
            cosine[here, :] = jnp.where(is_key, jnp.cos(angles), 1.0)
            turn = jnp.sin(angles)
            turn = jnp.where(lane < HEAD_WIDTH // 2, -turn, turn)
            sine[here, :] = jnp.where(is_key, turn, 0.0)

            @pl.when((me > 0) & (me < n - 1))
            def _():
                @pl.loop(0, n)
                def _(i):
                    j = n - 1 - i

                    @pl.when(j > me)
                    def _():
                        rightward(b, j).wait_recv()
                        add_arrived(b, j, from_left)
                        rightward(b, j).start()

                    @pl.when(i < me)
                    def _():
                        leftward(b, i).wait_recv()
                        add_arrived(b, i, from_right)
                        leftward(b, i).start()

        @pl.when(step >= early)
        def _():
            b = step - early

            @pl.when(me > 0)
            def _():
                rightward(b, me).wait_recv()
                add_arrived(b, me, from_left)

            @pl.when(me < n - 1)
            def _():
                leftward(b, me).wait_recv()
                add_arrived(b, me, from_right)

    @pl.loop(0, n)
    def _(peer):
        @pl.when(peer != me)
        def _():
            square_copy(peer, peer).wait_recv()
            square_copy(me, peer).wait_send()

    @pl.loop(0, blocks)
    def _(b):
        here = pl.ds(b * rows, rows)
        total = squares[0, :, here]
        for peer in range(1, n):
            total = total + squares[peer, :, here]
        inverse_rms = jnp.transpose(lax.rsqrt(total / MODEL_WIDTH + EPSILON))[:, 0:1]
        place = lax.broadcasted_iota(jnp.int32, (rows, HEAD_WIDTH), 0) + b * rows
        live = place < limit[...]
        for head in range(columns // HEAD_WIDTH):
            own = slice(head * HEAD_WIDTH, (head + 1) * HEAD_WIDTH)
            normed = partial[b, me, :, own].astype(jnp.float32) * inverse_rms
            turned = pltpu.roll(normed, HEAD_WIDTH // 2, 1)
            rotated = normed * cosine[here, :] + turned * sine[here, :]
            result[here, own] = jnp.where(live, rotated, 0.0).astype(jnp.bfloat16)

    @pl.loop(0, blocks)
    def _(b):
        @pl.loop(0, n)
        def _(j):
            @pl.when(j > me)
            def _():
                rightward(b, j).wait_send()

            @pl.when(j < me)
            def _():
                leftward(b, j).wait_send()


def body(hidden, lengths, adapter_index, gain, wkv, down_weights, key_up_weights, value_up_weights):
    my_replica = lax.axis_index("rep")
    n = lax.axis_size("tp")
    own_length = lengths[my_replica]
    adapter = adapter_index[my_replica]
    key_columns = key_up_weights.shape[1]
    width = hidden.shape[1]
    row_count = hidden.shape[0]
    columns = wkv.shape[1] // n
    adapters = key_up_weights.shape[0] // ADAPTER_RANK
    mine = (jnp.arange(adapters) == adapter)[:, None, None]
    key_up = jnp.where(mine, key_up_weights.reshape(adapters, ADAPTER_RANK, -1), 0)
    value_up = jnp.where(mine, value_up_weights.reshape(adapters, ADAPTER_RANK, -1), 0)
    up = jnp.concatenate(
        [
            jnp.concatenate([key_up, jnp.zeros_like(value_up)], axis=2),
            jnp.concatenate([jnp.zeros_like(key_up), value_up], axis=2),
        ],
        axis=1,
    ).reshape(down_weights.shape[1], wkv.shape[1])
    rows = 2 * SPAN
    blocks = row_count // rows
    vmem = pl.BlockSpec(memory_space=pltpu.VMEM)
    chunk_buffer = pltpu.VMEM((blocks, n, rows, columns), jnp.bfloat16)
    chunk_semaphores = pltpu.SemaphoreType.DMA((blocks, n))
    index = jnp.arange(HEAD_WIDTH // 2, dtype=jnp.float32)
    frequency = jnp.tile(jnp.power(jnp.float32(THETA), -2.0 * index / HEAD_WIDTH), 2)[None, :]
    limit = jnp.full((1, HEAD_WIDTH), own_length * SPAN, jnp.int32)
    return pl.pallas_call(
        functools.partial(kernel, n, blocks, rows, columns, key_columns),
        out_shape=jax.ShapeDtypeStruct((row_count, columns), jnp.bfloat16),
        in_specs=[vmem] * 7,
        out_specs=vmem,
        scratch_shapes=[
            pltpu.VMEM((rows, width), jnp.bfloat16),
            pltpu.VMEM((row_count, HEAD_WIDTH), jnp.float32),
            pltpu.VMEM((row_count, HEAD_WIDTH), jnp.float32),
            chunk_buffer,
            chunk_buffer,
            chunk_buffer,
            pltpu.VMEM((n, 8, row_count), jnp.float32),
            chunk_semaphores,
            chunk_semaphores,
            chunk_semaphores,
            chunk_semaphores,
            pltpu.SemaphoreType.DMA((n,)),
            pltpu.SemaphoreType.DMA((n,)),
        ],
        compiler_params=pltpu.CompilerParams(
            collective_id=0, has_side_effects=True, vmem_limit_bytes=60 * 1024 * 1024
        ),
    )(hidden, gain[None, :], wkv, down_weights, up, frequency, limit)


def solution(mesh):
    return jax.shard_map(
        body,
        mesh=mesh,
        in_specs=(
            P(("outer", "rep"), "tp"),
            P("outer"),
            P("outer"),
            P("tp"),
            P("tp", None),
            P("tp", None),
            P(),
            P(),
        ),
        out_specs=P(("outer", "rep"), "tp"),
        check_vma=False,
    )
```
